256 devices in a mesh: dp: 32 (over y, z_hi, core), tensor: 8 (over x, z_lo).
Axes of the slice: x: 4, y: 4, z: 8 (z_hi: 4, z_lo: 2; z = z_hi * 2 + z_lo), core: 2. Of those that a mesh axis runs over, the one named last changes fastest.
Arguments:
- prefix_cache: bfloat16 [32, 2048, 2048], P('dp', None, 'tensor'), may hold values from -6 to 6
- prefix_len: int32 [32], P('dp'), may hold values from 1 to 2048, 40960 in all
- decode_q: bfloat16 [512, 4096], P('dp', 'tensor'), may hold values from -130 to 130
- sample_kv: bfloat16 [512, 2048], P('dp', 'tensor'), may hold values from -6 to 6
- sample_count: int32 [32], P('dp'), may hold values from 1 to 16, 384 in all
- sectioned_pages: bfloat16 [768, 128, 2048], P('dp', None, 'tensor'), may hold values from -6 to 6
- page_owner: int32 [768, 1], P('dp'), may hold values from 0 to 31; in each aligned block of 24 rows (0 to 23, 24 to 47, ...) at most 2 rows name the same one
- prefill_q: bfloat16 [65536, 4096], P('dp', 'tensor'), may hold values from -130 to 130
- prefill_kv: bfloat16 [65536, 2048], P('dp', 'tensor'), may hold values from -6 to 6
- span_len: int32 [32], P('dp'), may hold values from 1 to 2048, 40960 in all
- out_weight: bfloat16 [4096, 4096], P('tensor'), may hold values from -0.09375 to 0.09375
Outputs:
- decode_out: bfloat16 [512, 4096], P('dp', 'tensor')
- prefill_out: bfloat16 [65536, 4096], P('dp', 'tensor')
The draws below stay inside these ranges and needn't reach their ends.
Inputs may be any that keep to these rules, and one draw needn't show every extreme that they name: `page_owner`: in the 24 sectioned pages of one group no prompt is named more than 2 times.
All inputs are finite; a program needn't handle non-finite values. No bound on the sum of `prefix_len` or of `sample_count` or of `span_len` on one device may be relied on, other than what follows from the above.
Results may differ from the reference program's by a relative error of at most 0.019.
Values may be sent and summed in bfloat16 or wider, within the bound.
A program may use at most 64 MiB of HBM per device.

```python
import math
import jax
import jax.numpy as jnp
import numpy as np
from jax import lax

HD = 128
KVH = 8
HQ = 32
D_WIN = 4096
PAGE = 128
SAMPLES = 16
MOST = 2
PAGES_DEV = 24
PREFIX = 2048
SPAN = 2048
N_DP = 32


def prefix_base(key):
    key = jax.random.fold_in(key, 103)
    return jnp.clip(jax.random.normal(key, (N_DP, PREFIX, KVH * 2 * HD), jnp.float32), -6.0, 6.0)


def prefill_base(key):
    key = jax.random.fold_in(key, 101)
    return jnp.clip(jax.random.normal(key, (N_DP * SPAN, KVH * 2 * HD), jnp.float32), -6.0, 6.0)


def draw_prefix_cache(key, part):
    return prefix_base(key).astype(jnp.bfloat16)


def draw_prefill_kv(key, part):
    return prefill_base(key).astype(jnp.bfloat16)


def draw_sectioned_pages(key, part):
    key = jax.random.fold_in(key, 107)
    count = N_DP * PAGES_DEV
    base = jnp.clip(jax.random.normal(key, (count, PAGE, KVH * 2 * HD), jnp.float32), -6.0, 6.0)
    return base.astype(jnp.bfloat16)


def draw_decode_q(key, part):
    key = jax.random.fold_in(key, 7)
    rows = N_DP * SAMPLES
    values = 2.0 * jnp.clip(jax.random.normal(key, (rows, HQ * HD), jnp.float32), -6.0, 6.0)
    return values.astype(jnp.bfloat16)


def draw_prefill_q(key, part):
    key = jax.random.fold_in(key, 11)
    rows = N_DP * SPAN
    values = 2.0 * jnp.clip(jax.random.normal(key, (rows, HQ * HD), jnp.float32), -6.0, 6.0)
    return values.astype(jnp.bfloat16)


def block_scale(rng, extent, shards, low, high):
    def one(position, shards_of):
        steps = jax.random.uniform(jax.random.fold_in(jax.random.fold_in(rng, 6), position), (shards_of,), jnp.float32, low / len(shards), high / len(shards))
        return jnp.repeat(jnp.exp(steps), extent[position] // shards_of).reshape((-1,) + (1,) * (len(extent) - position - 1))

    gain = one(*shards[0])
    for cut in shards[1:]:
        gain = gain * one(*cut)
    return gain


def profile(number_of, total, bound, slope):
    loads = [(1 << 20) // math.isqrt(rank ** slope) + 1 for rank in range(2, number_of + 1)]
    rest, given = total - bound - (number_of - 1), [1] * (number_of - 1)
    while rest > 0:
        free = [i for i in range(number_of - 1) if given[i] < bound]
        mass, remaining = sum([loads[i] for i in free]), rest
        for i in free:
            extra = min(bound - given[i], max(1, remaining * loads[i] // mass), rest)
            given[i] = given[i] + extra
            rest = rest - extra
    return np.array([bound] + given)


def ragged(key, number_of, total, most, skew):
    if number_of == 2:
        one = jax.random.randint(key, (), max(1, total - most), min(most, total - 1) + 1)
        return jnp.stack([one, total - one])
    tallies = jnp.asarray(profile(number_of, total, most, skew), jnp.int32)
    twos = (number_of - 1) // 2
    donor, receiver = tallies[1:1 + 2 * twos:2], tallies[2:2 + 2 * twos:2]
    margin = jnp.minimum(donor - 1, most - receiver)
    shifted = jax.random.randint(jax.random.fold_in(key, 1), (twos,), 0, 1 << 20) % (margin + 1)
    tallies = tallies.at[1:1 + 2 * twos:2].set(donor - shifted).at[2:2 + 2 * twos:2].set(receiver + shifted)
    return tallies[jax.random.permutation(jax.random.fold_in(key, 2), number_of)]


def shared_out(own_key, own, number, rows, count, top, most, skew):
    ranking = jax.random.permutation(own_key, count)
    packed, common = load_shares(count, rows * top, most, skew, True), load_shares(count, rows * top, most, skew, False)
    places = jnp.arange(count)

    def named(tallies, rotation):
        used = int((tallies > 0).sum())
        fixed = max(1, used // 4)
        passed = fixed + (places - fixed + rotation * (used - fixed)) % max(1, count - fixed)
        return jnp.zeros((count,), jnp.int32).at[ranking[jnp.where(places < fixed, places, passed)]].set(jnp.asarray(tallies, jnp.int32))

    tallies = jnp.where(number % 4 == 0, named(packed, number // 4), named(common, number - number // 4 - 1))
    mixed = jax.random.permutation(jax.random.fold_in(own, 3), count)
    source_of, sink = mixed[0:count // 2 * 2:2], mixed[1:count // 2 * 2:2]
    room = jnp.minimum(tallies[source_of] - 1, most - tallies[sink]) // 2
    room = jnp.where((source_of == ranking[0]) | (sink == ranking[0]) | (tallies[sink] == 0), 0, jnp.maximum(room, 0))
    passed = jax.random.randint(jax.random.fold_in(own, 4), (count // 2,), 0, 1 << 20) % (room + 1)
    tallies = tallies.at[source_of].add(-passed).at[sink].add(passed)
    members = jnp.searchsorted(jnp.cumsum(tallies), jnp.arange(rows * top), side="right").astype(jnp.int32)
    grid = members.reshape(top, rows).T
    grid = grid[jax.random.permutation(jax.random.fold_in(own, 1), rows)]
    rotation = jax.random.randint(jax.random.fold_in(own, 2), (rows, 1), 0, top)
    return jnp.take_along_axis(grid, (jnp.arange(top)[None, :] + rotation) % top, axis=1)


def load_shares(amount, total, bound, skew, full):
    loads = [(1 << 20) // math.isqrt(grade ** skew) + 1 for grade in range(1, amount + 1)]
    largest = bound if full else min(bound, max(-(-total // amount), total * loads[0] // sum(loads)))
    least = 1 if total - largest >= amount - 1 else 0
    counts, rest = [largest] + [least] * (amount - 1), total - largest - least * (amount - 1)
    while rest > 0:
        candidates = [i for i in range(1, amount) if counts[i] < largest] or [i for i in range(1, amount) if counts[i] < bound]
        pool, budget = sum([loads[i] for i in candidates]), rest
        for i in candidates:
            more = min(bound - counts[i], max(1, budget * loads[i] // pool), rest)
            counts[i] = counts[i] + more
            rest = rest - more
    return np.array(counts)


def scatter_about(rng, extent, scale, most, pieces=(), held_as=jnp.bfloat16):
    values = jax.random.normal(rng, extent, jnp.float32) * scale
    if len(pieces) > 0:
        values = block_scale(rng, extent, pieces, -0.22, 0.18) * values
    return jnp.clip(values, min=-most, max=most).astype(held_as)


def setup_inputs(seed: int = 0) -> dict:
    key_of = jax.random.split(jax.random.key(seed), 12)
    prefix_cache = draw_prefix_cache(jax.random.fold_in(key_of[11], 71), 0)
    prefix_len = ragged(key_of[1], N_DP, N_DP * PREFIX * 5 // 8, PREFIX, 1).astype(jnp.int32)
    decode_q = draw_decode_q(jax.random.fold_in(key_of[11], 71), 0)
    sample_kv = scatter_about(key_of[3], (N_DP * SAMPLES, KVH * 2 * HD), 1.0, 6.0, ((0, 32), (1, 8)))
    sample_count = ragged(key_of[4], N_DP, N_DP * SAMPLES * 3 // 4, SAMPLES, 1).astype(jnp.int32)
    sectioned_pages = draw_sectioned_pages(jax.random.fold_in(key_of[11], 71), 0)
    page_owner_keys = jax.random.split(jax.random.fold_in(key_of[6], 1), (N_DP * PAGES_DEV) // PAGES_DEV)
    page_owner_turns = jax.random.permutation(jax.random.fold_in(key_of[6], 3), (N_DP * PAGES_DEV) // PAGES_DEV)
    page_owner = jax.vmap(lambda own, number: shared_out(jax.random.fold_in(key_of[6], 2), own, number, PAGES_DEV, N_DP, 1, MOST, 1))(page_owner_keys, page_owner_turns).reshape((N_DP * PAGES_DEV, 1))
    prefill_q = draw_prefill_q(jax.random.fold_in(key_of[11], 71), 0)
    prefill_kv = draw_prefill_kv(jax.random.fold_in(key_of[11], 71), 0)
    span_len = ragged(key_of[9], N_DP, N_DP * SPAN * 5 // 8, SPAN, 1).astype(jnp.int32)
    out_weight = scatter_about(key_of[10], (HQ * HD, D_WIN), (HQ * HD) ** -0.5, 0.09375, ((0, 8),))
    return {"prefix_cache": prefix_cache, "prefix_len": prefix_len, "decode_q": decode_q, "sample_kv": sample_kv, "sample_count": sample_count, "sectioned_pages": sectioned_pages, "page_owner": page_owner, "prefill_q": prefill_q, "prefill_kv": prefill_kv, "span_len": span_len, "out_weight": out_weight}


NEG = -1e+30

def rounded(values):
    return lax.optimization_barrier(values.astype(jnp.bfloat16)).astype(jnp.float32)

def reference(prefix_cache, prefix_len, decode_q, sample_kv, sample_count, sectioned_pages, page_owner, prefill_q, prefill_kv, span_len, out_weight):
    factor = 1.0 / math.sqrt(HD)
    per_kv = HQ // KVH
    queries = decode_q.astype(jnp.float32).reshape(N_DP, SAMPLES, KVH, per_kv, HD)
    own = sample_kv.astype(jnp.float32).reshape(N_DP, SAMPLES, KVH, 2, HD)

    def prefix_scores(cache, length, query, mine):
        cache32 = cache.astype(jnp.float32).reshape(PREFIX, KVH, 2, HD)
        scores = jnp.einsum('shgd,thd->shgt', query, cache32[:, :, 0]) * factor
        live = jnp.arange(PREFIX) < length
        scores = jnp.where(live[None, None, None, :], scores, NEG)
        own_score = jnp.einsum('shgd,shd->shg', query, mine[:, :, 0]) * factor
        return (scores, own_score, cache32)

    def prefix_top(args):
        scores, own_score, unused = prefix_scores(*args)
        return jnp.maximum(scores.max(-1), own_score)
    tops = lax.map(prefix_top, (prefix_cache, prefix_len, queries, own))
    pages = sectioned_pages.reshape(N_DP, PAGES_DEV, PAGE, KVH, 2, HD)
    owners = page_owner.reshape(N_DP, PAGES_DEV)
    groups_iota = jnp.arange(N_DP)

    def page_scores(block, owner):
        keyvals = block.astype(jnp.float32)
        scores = jnp.einsum('pshgd,pthd->pshgt', queries[owner], keyvals[:, :, :, 0, :]) * factor
        return (scores, keyvals)

    def max_step(top, inputs):
        block, owner = inputs
        scores, unused = page_scores(block, owner)
        page_max = scores.max(-1)
        hit = groups_iota[:, None] == owner[None, :]
        candidate = jnp.where(hit[:, :, None, None, None], page_max[None], NEG).max(1)
        return (jnp.maximum(top, candidate), None)
    page_top, unused = lax.scan(max_step, jnp.full((N_DP, SAMPLES, KVH, per_kv), NEG, jnp.float32), (pages, owners))
    top = jnp.maximum(tops, page_top)

    def sum_step(carry, inputs):
        l_sum, acc_sum = carry
        block, owner = inputs
        scores, keyvals = page_scores(block, owner)
        weights = jnp.exp(scores - top[owner][..., None])
        totals = weights.sum(-1)
        acc = jnp.einsum('pshgt,pthd->pshgd', rounded(weights), keyvals[:, :, :, 1, :])
        hit = (groups_iota[:, None] == owner[None, :]).astype(jnp.float32)
        l_sum = l_sum + jnp.einsum('np,pshg->nshg', hit, totals, precision=lax.Precision.HIGHEST)
        acc_sum = acc_sum + jnp.einsum('np,pshgd->nshgd', hit, acc, precision=lax.Precision.HIGHEST)
        return ((l_sum, acc_sum), None)
    start_l = jnp.zeros((N_DP, SAMPLES, KVH, per_kv), jnp.float32)
    start_acc = jnp.zeros((N_DP, SAMPLES, KVH, per_kv, HD), jnp.float32)
    (l_page, acc_page), unused = lax.scan(sum_step, (start_l, start_acc), (pages, owners))

    def prefix_sums(args):
        cache, length, query, mine, top_group = args
        scores, own_score, cache32 = prefix_scores(cache, length, query, mine)
        weights = jnp.exp(scores - top_group[..., None])
        own_weight = jnp.exp(own_score - top_group)
        totals = weights.sum(-1) + own_weight
        acc = jnp.einsum('shgt,thd->shgd', rounded(weights), cache32[:, :, 1])
        acc = acc + rounded(own_weight)[..., None] * mine[:, :, 1][:, :, None, :]
        return (totals, acc)
    l_pre, acc_pre = lax.map(prefix_sums, (prefix_cache, prefix_len, queries, own, top))
    attended = ((acc_pre + acc_page) / (l_pre + l_page)[..., None]).astype(jnp.bfloat16).reshape(N_DP * SAMPLES, HQ * HD)
    projected = jnp.dot(attended, out_weight, preferred_element_type=jnp.float32)
    alive = (jnp.arange(SAMPLES)[None, :] < sample_count[:, None]).reshape(-1)
    decode_out = jnp.where(alive[:, None], projected, 0.0).astype(jnp.bfloat16)
    rows = jnp.arange(SPAN)
    causal = rows[None, :] <= rows[:, None]

    def prefill_span(args):
        query, pair, length = args
        q32 = query.astype(jnp.float32).reshape(SPAN, KVH, per_kv, HD)
        kv32 = pair.astype(jnp.float32).reshape(SPAN, KVH, 2, HD)

        def one_head(head_args):
            head_q, head_k, head_v = head_args
            scores = jnp.einsum('rgd,kd->grk', head_q, head_k) * factor
            scores = jnp.where(causal[None], scores, NEG)
            weights = jnp.exp(scores - scores.max(-1, keepdims=True))
            totals = weights.sum(-1)
            result = jnp.einsum('grk,kd->rgd', rounded(weights), head_v)
            return result / totals.T[:, :, None]
        outputs = lax.map(one_head, (q32.transpose(1, 0, 2, 3), kv32[:, :, 0].transpose(1, 0, 2), kv32[:, :, 1].transpose(1, 0, 2)))
        outputs = outputs.transpose(1, 0, 2, 3).reshape(SPAN, HQ * HD)
        outputs = jnp.where((rows < length)[:, None], outputs, 0.0)
        return outputs.astype(jnp.bfloat16)
    prefill_out = lax.map(prefill_span, (prefill_q.reshape(N_DP, SPAN, HQ * HD), prefill_kv.reshape(N_DP, SPAN, KVH * 2 * HD), span_len))
    return (decode_out, prefill_out.reshape(N_DP * SPAN, HQ * HD))
```

```python
import functools
import math

import jax
import jax.numpy as jnp
from jax import lax
from jax.experimental import pallas as pl
from jax.experimental.pallas import tpu as pltpu
from jax.sharding import PartitionSpec as P

MESH = pl.DeviceIdType.MESH
HD = 128
HEADS = 4
NEG = -1e30
SCALE = math.log2(math.e) / math.sqrt(HD)
GRID_Z = 4
BLOCK = 256


def nt_dot(a, b):
    return lax.dot_general(a, b, (((1,), (1,)), ((), ())), preferred_element_type=jnp.float32)


def nn_dot(a, b):
    return jnp.dot(a, b, preferred_element_type=jnp.float32)


def kernel(
    chips_z,
    plen_ref, scount_ref, slen_ref, owner_ref, dq_ref, skv_ref,
    prefix_hbm, pages_hbm, pq_hbm, pkv_hbm, w_hbm,
    dec_out, pre_out,
    prefix, pages, pq, pkv, w, po, kt, v1,
    table, table_sib, tab_s, tab_sib_s,
    q_all, acc_send, st_send, acc_recv, st_recv, part, rs_recv, dec,
    in_sem, out_sem, tab_sem, swap_send, swap_recv,
    q_send, q_recv, a_send, a_recv, t_send, t_recv, r_send, r_recv,
):
    span = pq.shape[0]
    pages_dev = pages_hbm.shape[0]
    samples = dq_ref.shape[0]
    rows = samples * HEADS
    chips = q_all.shape[0]
    chips_y = chips // chips_z
    n_t = rs_recv.shape[0]
    dp = lax.axis_index("dp")
    me_t = lax.axis_index("tensor")
    chip, core = dp // 2, dp % 2
    sibling = chip * 2 + (1 - core)
    my_y, my_z = chip // chips_z, chip % chips_z

    order = sorted(
        range(chips),
        key=lambda r: (min(r // chips_z, chips_y - r // chips_z) + 2 * min(r % chips_z, chips_z - r % chips_z), r),
    )

    def forward(r):
        return ((my_y + r // chips_z) % chips_y) * chips_z + (my_z + r % chips_z) % chips_z

    def backward(r):
        return ((my_y + chips_y - r // chips_z) % chips_y) * chips_z + (my_z + chips_z - r % chips_z) % chips_z

    barrier = pltpu.get_barrier_semaphore()
    for r in range(1, chips):
        pl.semaphore_signal(barrier, inc=1, device_id=(forward(r) * 2 + core, me_t), device_id_type=MESH)
    for u in range(1, n_t):
        pl.semaphore_signal(barrier, inc=1, device_id=(dp, (me_t + u) % n_t), device_id_type=MESH)
    pl.semaphore_signal(barrier, inc=1, device_id=(sibling, me_t), device_id_type=MESH)

    load_kv = pltpu.make_async_copy(pkv_hbm, pkv, in_sem.at[0])
    load_q = pltpu.make_async_copy(pq_hbm, pq, in_sem.at[1])
    load_prefix = pltpu.make_async_copy(prefix_hbm.at[0], prefix, in_sem.at[2])
    load_pages = pltpu.make_async_copy(pages_hbm, pages.at[pl.ds(0, pages_dev)], in_sem.at[3])
    load_w = pltpu.make_async_copy(w_hbm, w, in_sem.at[4])
    for copy in (load_kv, load_q, load_pages, load_prefix, load_w):
        copy.start()

    place = lax.broadcasted_iota(jnp.int32, (pages_dev, 128), 0)
    lane = lax.broadcasted_iota(jnp.int32, (pages_dev, 128), 1)
    hit = owner_ref[...] == lane
    first = jnp.min(jnp.where(hit, place, pages_dev), axis=0, keepdims=True)
    last = jnp.max(jnp.where(hit, place, -1), axis=0, keepdims=True)
    row8 = lax.broadcasted_iota(jnp.int32, (8, 128), 0)
    table[...] = jnp.where(row8 == 0, first, last)
    own_tab = pltpu.make_async_copy(table, tab_s, tab_sem.at[0])
    own_tab.start()

    load_kv.wait()
    ktt = pkv[:, :HD].T
    kt[:HD, :] = ktt
    kt[HD:, :] = ktt
    v1[:, :HD] = pkv[:, HD:]
    v1[:, HD:] = jnp.ones((span, HD), jnp.bfloat16)
    load_q.wait()
    length = slen_ref[0]
    block = min(BLOCK, span)
    n_blocks = span // block
    tri = lax.broadcasted_iota(jnp.int32, (block, block), 1) <= lax.broadcasted_iota(jnp.int32, (block, block), 0)

    def prefill(i):
        lo, nk = i * block, (i + 1) * block
        live = lo + lax.broadcasted_iota(jnp.int32, (block, HD), 0) < length
        for h in range(HEADS):
            q = pq[lo:nk, h * HD:(h + 1) * HD].astype(jnp.float32) * SCALE
            q_hi = q.astype(jnp.bfloat16)
            q_lo = (q - q_hi.astype(jnp.float32)).astype(jnp.bfloat16)
            s = nn_dot(jnp.concatenate([q_hi, q_lo], axis=1), kt[:, :nk])
            diag = jnp.where(tri, s[:, lo:], NEG)
            s = jnp.concatenate([s[:, :lo], diag], axis=1) if i else diag
            top = jnp.max(s, axis=1, keepdims=True)
            p = jnp.exp2(s - top).astype(jnp.bfloat16)
            o = nn_dot(p, v1[:nk, :])
            out = jnp.where(live, o[:, :HD] / o[:, HD:], 0.0)
            po[lo:nk, h * HD:(h + 1) * HD] = out.astype(jnp.bfloat16)
        pltpu.make_async_copy(po.at[pl.ds(lo, block)], pre_out.at[pl.ds(lo, block)], out_sem.at[i]).start()

    sequence = list(range(n_blocks))
    cut_a, cut_b, cut_c = 3 * n_blocks // 8, 5 * n_blocks // 8, 7 * n_blocks // 8
    for i in sequence[:cut_a]:
        prefill(i)

    pl.semaphore_wait(barrier, chips - 1 + n_t - 1 + 1)
    swap = [
        pltpu.make_async_remote_copy(
            table, table_sib, swap_send.at[0], swap_recv.at[0], device_id=(sibling, me_t), device_id_type=MESH),
        pltpu.make_async_remote_copy(
            pages_hbm, pages.at[pl.ds(pages_dev, pages_dev)], swap_send.at[1], swap_recv.at[1],
            device_id=(sibling, me_t), device_id_type=MESH),
    ]

    def q_copy(r):
        return pltpu.make_async_remote_copy(
            dq_ref, q_all.at[r], q_send.at[r], q_recv.at[r],
            device_id=(forward(r) * 2 + core, me_t), device_id_type=MESH)

    swap[0].start()
    for r in order[::-1]:
        if r:
            q_copy(r).start()
    swap[1].start()

    def stacked(x):
        return jnp.concatenate([x[:, h * HD:(h + 1) * HD] for h in range(HEADS)], axis=0)

    dq = stacked(dq_ref[...])
    load_prefix.wait()
    n_prefix = prefix.shape[0]
    s = nt_dot(dq, prefix[:, :HD]) * SCALE
    at = lax.broadcasted_iota(jnp.int32, (rows, n_prefix), 1)
    s = jnp.where(at < plen_ref[0], s, NEG)
    own_k = jnp.concatenate([skv_ref[:, :HD].astype(jnp.float32)] * HEADS, axis=0)
    own_v = jnp.concatenate([skv_ref[:, HD:].astype(jnp.float32)] * HEADS, axis=0)
    own_s = jnp.sum(dq.astype(jnp.float32) * own_k, axis=1, keepdims=True) * SCALE
    m_pre = jnp.maximum(jnp.max(s, axis=1, keepdims=True), own_s)
    p = jnp.exp2(s - m_pre)
    own_w = jnp.exp2(own_s - m_pre)
    l_pre = jnp.sum(p, axis=1, keepdims=True) + own_w
    acc_pre = nn_dot(p.astype(jnp.bfloat16), prefix[:, HD:])
    acc_pre = acc_pre + own_w.astype(jnp.bfloat16).astype(jnp.float32) * own_v

    for i in sequence[cut_a:cut_b]:
        prefill(i)

    load_pages.wait()
    own_tab.wait()
    swap[0].wait()
    sib_tab = pltpu.make_async_copy(table_sib, tab_sib_s, tab_sem.at[1])
    sib_tab.start()
    sib_tab.wait()
    swap[1].wait()
    ones = jnp.ones((pages.shape[1], HD), jnp.bfloat16)
    lane_r = lax.broadcasted_iota(jnp.int32, (rows, 128), 1)
    row_r = lax.broadcasted_iota(jnp.int32, (rows, 128), 0)

    def a_copy(r):
        return pltpu.make_async_remote_copy(
            acc_send.at[r], acc_recv.at[r], a_send.at[r], a_recv.at[r],
            device_id=(backward(r) * 2 + core, me_t), device_id_type=MESH)

    def t_copy(r):
        return pltpu.make_async_remote_copy(
            st_send.at[r], st_recv.at[r], t_send.at[r], t_recv.at[r],
            device_id=(backward(r) * 2 + core, me_t), device_id_type=MESH)

    def serve(r):
        q = stacked(q_all[r]) if r else dq
        prompt = backward(r) * 2 + core
        held = []
        for tab, base in ((tab_s, 0), (tab_sib_s, pages_dev)):
            a, b = tab[0, prompt], tab[1, prompt]
            held.append((base + jnp.minimum(a, pages_dev - 1), b >= a))
            held.append((base + jnp.maximum(b, 0), b > a))
        kvs = [pages[index] for index, _ in held]
        s = jnp.concatenate(
            [nt_dot(q, kv[:, :HD]) * SCALE + jnp.where(valid, 0.0, NEG)
             for kv, (_, valid) in zip(kvs, held)], axis=1)
        m = jnp.max(s, axis=1, keepdims=True)
        p = jnp.exp2(s - m).astype(jnp.bfloat16)
        v = jnp.concatenate([jnp.concatenate([kv[:, HD:], ones], axis=1) for kv in kvs], axis=0)
        o = nn_dot(p, v)
        stat = jnp.where(lane_r == row_r, m, jnp.where(lane_r == row_r + rows, o[:, HD:], 0.0))
        stat = jnp.sum(stat, axis=0, keepdims=True)
        if r:
            acc_send[r] = o[:, :HD].astype(jnp.bfloat16)
            st_send[r] = stat
        else:
            acc_recv[0] = o[:, :HD].astype(jnp.bfloat16)
            st_recv[0] = stat

    for start in range(0, chips, 4):
        group = order[start:start + 4]
        for r in group:
            if r:
                q_copy(r).wait_recv()
        for r in group:
            serve(r)
        for r in group:
            if r:
                t_copy(r).start()
                a_copy(r).start()

    for i in sequence[cut_c:] + sequence[cut_b:cut_c - 1]:
        prefill(i)

    for r in range(1, chips):
        t_copy(r).wait_recv()
        a_copy(r).wait_recv()
    stats = jnp.concatenate([st_recv[r] for r in range(chips)], axis=0).T
    m_all, l_all = stats[:rows, :], stats[rows:2 * rows, :]
    m_top = jnp.maximum(jnp.max(m_all, axis=1, keepdims=True), m_pre)
    w_all = jnp.exp2(m_all - m_top)
    w_pre = jnp.exp2(m_pre - m_top)
    total = jnp.sum(l_all * w_all, axis=1, keepdims=True) + l_pre * w_pre
    acc = acc_pre * w_pre
    for r in range(chips):
        acc = acc + acc_recv[r].astype(jnp.float32) * w_all[:, r:r + 1]
    att = (acc / total).astype(jnp.bfloat16)
    att = jnp.concatenate([att[h * samples:(h + 1) * samples, :] for h in range(HEADS)], axis=1)

    load_w.wait()
    wide = dec.shape[1]
    for b in range(n_t):
        part[b] = nn_dot(att, w[:, b * wide:(b + 1) * wide]).astype(jnp.bfloat16)

    def r_copy(u):
        to = (me_t + u) % n_t
        return pltpu.make_async_remote_copy(
            part.at[to], rs_recv.at[u], r_send.at[u], r_recv.at[u], device_id=(dp, to), device_id_type=MESH)

    for u in range(1, n_t):
        r_copy(u).start()

    for i in sequence[cut_c - 1:cut_c]:
        prefill(i)

    sums = part[me_t].astype(jnp.float32)
    for u in range(1, n_t):
        r_copy(u).wait_recv()
        sums = sums + rs_recv[u].astype(jnp.float32)
    alive = lax.broadcasted_iota(jnp.int32, sums.shape, 0) < scount_ref[0]
    dec[...] = jnp.where(alive, sums, 0.0).astype(jnp.bfloat16)
    store = pltpu.make_async_copy(dec, dec_out, out_sem.at[n_blocks])
    store.start()

    for r in range(1, chips):
        q_copy(r).wait_send()
        t_copy(r).wait_send()
        a_copy(r).wait_send()
    for u in range(1, n_t):
        r_copy(u).wait_send()
    for i in range(n_blocks):
        pltpu.make_async_copy(
            po.at[pl.ds(i * block, block)], pre_out.at[pl.ds(i * block, block)], out_sem.at[i]).wait()
    store.wait()


def solution(mesh, chips_z=GRID_Z):
    chips = mesh.shape["dp"] // 2
    n_t = mesh.shape["tensor"]

    def body(prefix_cache, prefix_len, decode_q, sample_kv, sample_count, sectioned_pages, page_owner,
             prefill_q, prefill_kv, span_len, out_weight):
        n_prefix, wide_kv = prefix_cache.shape[1:]
        pages_dev, page, _ = sectioned_pages.shape
        span, wide_q = prefill_q.shape
        samples = decode_q.shape[0]
        rows = samples * HEADS
        features = out_weight.shape[1]
        bf, f32 = jnp.bfloat16, jnp.float32
        n_blocks = span // min(BLOCK, span)
        vmem, smem, hbm = (pl.BlockSpec(memory_space=m) for m in (pltpu.VMEM, pltpu.SMEM, pl.ANY))
        dma, vm = pltpu.SemaphoreType.DMA, pltpu.VMEM
        return pl.pallas_call(
            functools.partial(kernel, chips_z),
            out_shape=(
                jax.ShapeDtypeStruct((samples, features // n_t), bf),
                jax.ShapeDtypeStruct((span, wide_q), bf),
            ),
            in_specs=[smem] * 3 + [vmem] * 3 + [hbm] * 5,
            out_specs=(hbm, hbm),
            scratch_shapes=[
                vm((n_prefix, wide_kv), bf), vm((2 * pages_dev, page, wide_kv), bf),
                vm((span, wide_q), bf), vm((span, wide_kv), bf), vm(out_weight.shape, bf),
                vm((span, wide_q), bf), vm((2 * HD, span), bf), vm((span, 2 * HD), bf),
                vm((8, 128), jnp.int32), vm((8, 128), jnp.int32),
                pltpu.SMEM((8, 128), jnp.int32), pltpu.SMEM((8, 128), jnp.int32),
                vm((chips, samples, wide_q), bf), vm((chips, rows, HD), bf), vm((chips, 1, 128), f32),
                vm((chips, rows, HD), bf), vm((chips, 1, 128), f32),
                vm((n_t, samples, features // n_t), bf), vm((n_t, samples, features // n_t), bf),
                vm((samples, features // n_t), bf),
                dma((5,)), dma((n_blocks + 1,)), dma((2,)), dma((2,)), dma((2,)),
                dma((chips,)), dma((chips,)), dma((chips,)), dma((chips,)), dma((chips,)), dma((chips,)),
                dma((n_t,)), dma((n_t,)),
            ],
            compiler_params=pltpu.CompilerParams(
                collective_id=0, has_side_effects=True, vmem_limit_bytes=50 * 2**20),
            cost_estimate=pl.CostEstimate(flops=6 * 10**9, bytes_accessed=12 * 2**20, transcendentals=10**7),
        )(prefix_len, sample_count, span_len, page_owner, decode_q, sample_kv,
          prefix_cache, sectioned_pages, prefill_q, prefill_kv, out_weight)

    in_specs = (
        P("dp", None, "tensor"), P("dp"), P("dp", "tensor"), P("dp", "tensor"), P("dp"),
        P("dp", None, "tensor"), P("dp", None), P("dp", "tensor"), P("dp", "tensor"), P("dp"), P("tensor", None),
    )
    out_specs = (P("dp", "tensor"), P("dp", "tensor"))
    return jax.shard_map(body, mesh=mesh, in_specs=in_specs, out_specs=out_specs, check_vma=False)
```

```python
import functools
import math

import jax
import jax.numpy as jnp
from jax import lax
from jax.experimental import pallas as pl
from jax.experimental.pallas import tpu as pltpu
from jax.sharding import PartitionSpec as P

MESH = pl.DeviceIdType.MESH
HD = 128
HEADS = 4
NEG = -1e30
SCALE = math.log2(math.e) / math.sqrt(HD)
GRID_Z = 4
BLOCK = 256


def nt_dot(a, b):
    return lax.dot_general(a, b, (((1,), (1,)), ((), ())), preferred_element_type=jnp.float32)


def nn_dot(a, b):
    return jnp.dot(a, b, preferred_element_type=jnp.float32)


def kernel(
    chips_z,
    plen_hbm, scount_hbm, slen_hbm, owner_hbm, dq_hbm, skv_hbm,
    prefix_hbm, pages_hbm, pq_hbm, pkv_hbm, w_hbm,
    dec, po,
    plen_ref, scount_ref, slen_ref, owner_ref, dq_ref, skv_ref,
    prefix, pages, pq, pkv, w, kt, v1,
    table, table_sib, tab_s, tab_sib_s,
    q_all, acc_send, st_send, acc_recv, st_recv, part, rs_recv,
    in_sem, tab_sem, swap_send, swap_recv,
    q_send, q_recv, a_send, a_recv, t_send, t_recv, r_send, r_recv,
):
    span = pq.shape[0]
    pages_dev = pages_hbm.shape[0]
    samples = dq_ref.shape[0]
    rows = samples * HEADS
    chips = q_all.shape[0]
    chips_y = chips // chips_z
    n_t = rs_recv.shape[0]
    dp = lax.axis_index("dp")
    me_t = lax.axis_index("tensor")
    chip, core = dp // 2, dp % 2
    sibling = chip * 2 + (1 - core)
    my_y, my_z = chip // chips_z, chip % chips_z

    early_waves, late_waves = list(range(chips_z // 2)), list(range(chips_z // 2, chips_z))
    is_first = my_z == 0
    is_early = my_z < chips_z // 2
    is_late = my_z >= chips_z // 2

    def chip_at(k, z):
        return ((my_y + k) % chips_y) * chips_z + z

    def remote(k, z, action):
        if k:
            action(chip_at(k, z))
        else:
            pl.when(my_z != z)(lambda: action(chip_at(k, z)))

    far_first = sorted(range(chips_y), key=lambda k: -min(k, chips_y - k))
    everywhere = [(k, z) for z in late_waves + early_waves for k in far_first]

    barrier = pltpu.get_barrier_semaphore()
    for k, z in everywhere:
        remote(k, z, lambda to: pl.semaphore_signal(
            barrier, inc=1, device_id=(to * 2 + core, me_t), device_id_type=MESH))
    for u in range(1, n_t):
        pl.semaphore_signal(barrier, inc=1, device_id=(dp, (me_t + u) % n_t), device_id_type=MESH)
    pl.semaphore_signal(barrier, inc=1, device_id=(sibling, me_t), device_id_type=MESH)

    load_kv = pltpu.make_async_copy(pkv_hbm, pkv, in_sem.at[0])
    load_q = pltpu.make_async_copy(pq_hbm, pq, in_sem.at[1])
    load_prefix = pltpu.make_async_copy(prefix_hbm.at[0], prefix, in_sem.at[2])
    load_pages = pltpu.make_async_copy(pages_hbm, pages.at[pl.ds(0, pages_dev)], in_sem.at[3])
    load_w = pltpu.make_async_copy(w_hbm, w, in_sem.at[4])
    small = [
        pltpu.make_async_copy(src, dst, in_sem.at[5 + i])
        for i, (src, dst) in enumerate((
            (owner_hbm, owner_ref), (slen_hbm, slen_ref), (dq_hbm, dq_ref), (skv_hbm, skv_ref),
            (plen_hbm, plen_ref), (scount_hbm, scount_ref)))
    ]
    load_owner, load_slen, load_dq, load_skv, load_plen, load_scount = small
    for copy in (load_owner, load_slen, load_kv, load_dq, load_q, load_pages, load_skv, load_plen, load_prefix,
                 load_scount, load_w):
        copy.start()

    load_owner.wait()
    prompts = table.shape[0]
    place = lax.broadcasted_iota(jnp.int32, (prompts, pages_dev), 1).astype(jnp.float32)
    prompt_at = lax.broadcasted_iota(jnp.int32, (prompts, pages_dev), 0)
    hit = jnp.broadcast_to(owner_ref[...], (prompts, pages_dev)) == prompt_at
    first = jnp.min(jnp.where(hit, place, float(pages_dev)), axis=1, keepdims=True)
    last = jnp.max(jnp.where(hit, place, -1.0), axis=1, keepdims=True)
    column = lax.broadcasted_iota(jnp.int32, (prompts, 128), 1)
    table[...] = jnp.where(column == 0, first, last).astype(jnp.int32)
    own_tab = pltpu.make_async_copy(table, tab_s, tab_sem.at[0])
    own_tab.start()

    block = min(BLOCK, span)
    n_blocks = span // block
    tri = lax.broadcasted_iota(jnp.int32, (block, block), 1) <= lax.broadcasted_iota(jnp.int32, (block, block), 0)

    def prepare():
        load_kv.wait()
        load_q.wait()
        load_slen.wait()
        ktt = pkv[:, :HD].T
        kt[:HD, :] = ktt
        kt[HD:, :] = ktt
        v1[:, :HD] = pkv[:, HD:]
        v1[:, HD:] = jnp.ones((span, HD), jnp.bfloat16)

    def prefill(i):
        lo, nk = i * block, (i + 1) * block
        length = jnp.broadcast_to(slen_ref[...], (block, HD))
        live = lo + lax.broadcasted_iota(jnp.int32, (block, HD), 0) < length
        for h in range(HEADS):
            q = pq[lo:nk, h * HD:(h + 1) * HD].astype(jnp.float32) * SCALE
            q_hi = q.astype(jnp.bfloat16)
            q_lo = (q - q_hi.astype(jnp.float32)).astype(jnp.bfloat16)
            s = nn_dot(jnp.concatenate([q_hi, q_lo], axis=1), kt[:, :nk])
            diag = jnp.where(tri, s[:, lo:], NEG)
            s = jnp.concatenate([s[:, :lo], diag], axis=1) if i else diag
            top = jnp.max(s, axis=1, keepdims=True)
            p = jnp.exp2(s - top).astype(jnp.bfloat16)
            o = nn_dot(p, v1[:nk, :])
            out = jnp.where(live, o[:, :HD] / o[:, HD:], 0.0)
            po[lo:nk, h * HD:(h + 1) * HD] = out.astype(jnp.bfloat16)

    def prefills(when, blocks):
        def run():
            for i in blocks:
                prefill(i)
        pl.when(when)(run)

    prepare()
    for i in (0, 1):
        prefill(i)

    pl.semaphore_wait(barrier, chips - 1 + n_t - 1 + 1)
    load_dq.wait()
    swap = [
        pltpu.make_async_remote_copy(
            table, table_sib, swap_send.at[0], swap_recv.at[0], device_id=(sibling, me_t), device_id_type=MESH),
        pltpu.make_async_remote_copy(
            pages_hbm, pages.at[pl.ds(pages_dev, pages_dev)], swap_send.at[1], swap_recv.at[1],
            device_id=(sibling, me_t), device_id_type=MESH),
    ]

    def q_copy(to, slot):
        return pltpu.make_async_remote_copy(
            dq_ref, q_all.at[slot], q_send.at[to], q_recv.at[slot],
            device_id=(to * 2 + core, me_t), device_id_type=MESH)

    def send_queries():
        for k, z in everywhere:
            remote(k, z, lambda to: q_copy(to, chip).start())

    swap[0].start()
    send_queries()
    swap[1].start()
    q_all[chip] = dq_ref[...]

    def stacked(x):
        return jnp.concatenate([x[:, h * HD:(h + 1) * HD] for h in range(HEADS)], axis=0)

    dq = stacked(dq_ref[...])
    load_prefix.wait()
    load_skv.wait()
    load_plen.wait()
    n_prefix = prefix.shape[0]
    s = nt_dot(dq, prefix[:, :HD]) * SCALE
    at = lax.broadcasted_iota(jnp.int32, (rows, n_prefix), 1)
    s = jnp.where(at < jnp.broadcast_to(plen_ref[...], (rows, n_prefix)), s, NEG)
    own_k = jnp.concatenate([skv_ref[:, :HD].astype(jnp.float32)] * HEADS, axis=0)
    own_v = jnp.concatenate([skv_ref[:, HD:].astype(jnp.float32)] * HEADS, axis=0)
    own_s = jnp.sum(dq.astype(jnp.float32) * own_k, axis=1, keepdims=True) * SCALE
    m_pre = jnp.maximum(jnp.max(s, axis=1, keepdims=True), own_s)
    p = jnp.exp2(s - m_pre)
    own_w = jnp.exp2(own_s - m_pre)
    l_pre = jnp.sum(p, axis=1, keepdims=True) + own_w
    acc_pre = nn_dot(p.astype(jnp.bfloat16), prefix[:, HD:])
    acc_pre = acc_pre + own_w.astype(jnp.bfloat16).astype(jnp.float32) * own_v

    for i in (2, 3, 4):
        prefill(i)

    load_pages.wait()
    own_tab.wait()
    swap[0].wait()
    sib_tab = pltpu.make_async_copy(table_sib, tab_sib_s, tab_sem.at[1])
    sib_tab.start()
    sib_tab.wait()
    swap[1].wait()
    ones = jnp.ones((pages.shape[1], HD), jnp.bfloat16)
    lane_r = lax.broadcasted_iota(jnp.int32, (rows, 128), 1)
    row_r = lax.broadcasted_iota(jnp.int32, (rows, 128), 0)

    def a_copy(to, slot):
        return pltpu.make_async_remote_copy(
            acc_send.at[to], acc_recv.at[slot], a_send.at[to], a_recv.at[slot],
            device_id=(to * 2 + core, me_t), device_id_type=MESH)

    def t_copy(to, slot):
        return pltpu.make_async_remote_copy(
            st_send.at[to], st_recv.at[slot], t_send.at[to], t_recv.at[slot],
            device_id=(to * 2 + core, me_t), device_id_type=MESH)

    def serve(r):
        q = stacked(q_all[r])
        prompt = r * 2 + core
        held = []
        for tab, base in ((tab_s, 0), (tab_sib_s, pages_dev)):
            a, b = tab[prompt, 0], tab[prompt, 1]
            held.append((base + jnp.clip(a, 0, pages_dev - 1), b >= a))
            held.append((base + jnp.clip(b, 0, pages_dev - 1), b > a))
        kvs = [pages[index] for index, _ in held]
        s = jnp.concatenate(
            [nt_dot(q, kv[:, :HD]) * SCALE + jnp.where(valid, 0.0, NEG)
             for kv, (_, valid) in zip(kvs, held)], axis=1)
        m = jnp.max(s, axis=1, keepdims=True)
        p = jnp.exp2(s - m).astype(jnp.bfloat16)
        v = jnp.concatenate([jnp.concatenate([kv[:, HD:], ones], axis=1) for kv in kvs], axis=0)
        o = nn_dot(p, v)
        stat = jnp.where(lane_r == row_r, m, jnp.where(lane_r == row_r + rows, o[:, HD:], 0.0))
        stat = jnp.sum(stat, axis=0, keepdims=True)
        acc_send[r] = o[:, :HD].astype(jnp.bfloat16)
        st_send[r] = stat

    for z in early_waves + late_waves:
        for k in far_first:
            remote(k, z, lambda of: q_copy(of, of).wait_recv())
        for k in far_first:
            serve(chip_at(k, z))
        for k in far_first:
            remote(k, z, lambda to: t_copy(to, chip).start())
            remote(k, z, lambda to: a_copy(to, chip).start())
    acc_recv[chip] = acc_send[chip]
    st_recv[chip] = st_send[chip]
    for i in (5, 7):
        prefill(i)

    for k, z in everywhere:
        remote(k, z, lambda of: t_copy(of, of).wait_recv())
        remote(k, z, lambda of: a_copy(of, of).wait_recv())
    stats = jnp.concatenate([st_recv[r] for r in range(chips)], axis=0).T
    m_all, l_all = stats[:rows, :], stats[rows:2 * rows, :]
    m_top = jnp.maximum(jnp.max(m_all, axis=1, keepdims=True), m_pre)
    w_all = jnp.exp2(m_all - m_top)
    w_pre = jnp.exp2(m_pre - m_top)
    total = jnp.sum(l_all * w_all, axis=1, keepdims=True) + l_pre * w_pre
    acc = acc_pre * w_pre
    for r in range(chips):
        acc = acc + acc_recv[r].astype(jnp.float32) * w_all[:, r:r + 1]
    att = (acc / total).astype(jnp.bfloat16)
    att = jnp.concatenate([att[h * samples:(h + 1) * samples, :] for h in range(HEADS)], axis=1)

    load_w.wait()
    wide = dec.shape[1]

    def product(u):
        to = (me_t + u) % n_t
        return nn_dot(att, w[:, pl.ds(pl.multiple_of(to * wide, wide), wide)])

    def r_copy(u):
        return pltpu.make_async_remote_copy(
            part.at[u], rs_recv.at[u], r_send.at[u], r_recv.at[u],
            device_id=(dp, (me_t + u) % n_t), device_id_type=MESH)

    for u in range(1, n_t):
        part[u] = product(u).astype(jnp.bfloat16)
        r_copy(u).start()
    part[0] = product(0).astype(jnp.bfloat16)

    for i in (6,):
        prefill(i)

    sums = part[0].astype(jnp.float32)
    for u in range(1, n_t):
        r_copy(u).wait_recv()
        sums = sums + rs_recv[u].astype(jnp.float32)
    load_scount.wait()
    alive = lax.broadcasted_iota(jnp.int32, sums.shape, 0) < jnp.broadcast_to(scount_ref[...], sums.shape)
    dec[...] = jnp.where(alive, sums, 0.0).astype(jnp.bfloat16)

    for k, z in everywhere:
        remote(k, z, lambda to: q_copy(to, chip).wait_send())
        remote(k, z, lambda to: t_copy(to, chip).wait_send())
        remote(k, z, lambda to: a_copy(to, chip).wait_send())
    for u in range(1, n_t):
        r_copy(u).wait_send()


def store(dec, pre, dec_out, pre_out, sem):
    copies = [pltpu.make_async_copy(pre, pre_out, sem.at[0]), pltpu.make_async_copy(dec, dec_out, sem.at[1])]
    for copy in copies:
        copy.start()
    for copy in copies:
        copy.wait()


def solution(mesh, chips_z=GRID_Z):
    chips = mesh.shape["dp"] // 2
    n_t = mesh.shape["tensor"]

    def body(prefix_cache, prefix_len, decode_q, sample_kv, sample_count, sectioned_pages, page_owner,
             prefill_q, prefill_kv, span_len, out_weight):
        n_prefix, wide_kv = prefix_cache.shape[1:]
        pages_dev, page, _ = sectioned_pages.shape
        span, wide_q = prefill_q.shape
        samples = decode_q.shape[0]
        rows = samples * HEADS
        features = out_weight.shape[1]
        bf, f32 = jnp.bfloat16, jnp.float32
        hbm = pl.BlockSpec(memory_space=pltpu.HBM)
        prompts = mesh.shape["dp"]
        dma, vm = pltpu.SemaphoreType.DMA, pltpu.VMEM
        outs = pl.pallas_call(
            functools.partial(kernel, chips_z),
            out_shape=(
                vm((samples, features // n_t), bf),
                vm((span, wide_q), bf),
            ),
            in_specs=[hbm] * 11,
            out_specs=(pl.BlockSpec(memory_space=vm),) * 2,
            scratch_shapes=[
                vm((1, 1), jnp.int32), vm((1, 1), jnp.int32), vm((1, 1), jnp.int32),
                vm((1, pages_dev), jnp.int32), vm((samples, wide_q), bf), vm((samples, wide_kv), bf),
                vm((n_prefix, wide_kv), bf), vm((2 * pages_dev, page, wide_kv), bf),
                vm((span, wide_q), bf), vm((span, wide_kv), bf), vm(out_weight.shape, bf),
                vm((2 * HD, span), bf), vm((span, 2 * HD), bf),
                vm((prompts, 128), jnp.int32), vm((prompts, 128), jnp.int32),
                pltpu.SMEM((prompts, 128), jnp.int32), pltpu.SMEM((prompts, 128), jnp.int32),
                vm((chips, samples, wide_q), bf), vm((chips, rows, HD), bf), vm((chips, 1, 128), f32),
                vm((chips, rows, HD), bf), vm((chips, 1, 128), f32),
                vm((n_t, samples, features // n_t), bf), vm((n_t, samples, features // n_t), bf),
                dma((11,)), dma((2,)), dma((2,)), dma((2,)),
                dma((chips,)), dma((chips,)), dma((chips,)), dma((chips,)), dma((chips,)), dma((chips,)),
                dma((n_t,)), dma((n_t,)),
            ],
            compiler_params=pltpu.CompilerParams(
                collective_id=0, has_side_effects=True, vmem_limit_bytes=56 * 2**20),
            cost_estimate=pl.CostEstimate(flops=6 * 10**9, bytes_accessed=12 * 2**20, transcendentals=10**7),
        )(prefix_len[None], sample_count[None], span_len[None], page_owner.T, decode_q, sample_kv,
          prefix_cache, sectioned_pages, prefill_q, prefill_kv, out_weight)
        return pl.pallas_call(
            store,
            out_shape=tuple(jax.ShapeDtypeStruct(out.shape, out.dtype) for out in outs),
            in_specs=[pl.BlockSpec(memory_space=vm)] * 2,
            out_specs=(hbm, hbm),
            scratch_shapes=[dma((2,))],
        )(*(pltpu.with_memory_space_constraint(out, vm) for out in outs))

    in_specs = (
        P("dp", None, "tensor"), P("dp"), P("dp", "tensor"), P("dp", "tensor"), P("dp"),
        P("dp", None, "tensor"), P("dp", None), P("dp", "tensor"), P("dp", "tensor"), P("dp"), P("tensor", None),
    )
    out_specs = (P("dp", "tensor"), P("dp", "tensor"))
    return jax.shard_map(body, mesh=mesh, in_specs=in_specs, out_specs=out_specs, check_vma=False)
```

```python
import functools
import math

import jax
import jax.numpy as jnp
from jax import lax
from jax.experimental import pallas as pl
from jax.experimental.pallas import tpu as pltpu
from jax.sharding import PartitionSpec as P

MESH = pl.DeviceIdType.MESH
HD = 128
HEADS = 4
NEG = -1e30
SCALE = math.log2(math.e) / math.sqrt(HD)
GRID_Z = 4
BLOCK = 256


def nt_dot(a, b):
    return lax.dot_general(a, b, (((1,), (1,)), ((), ())), preferred_element_type=jnp.float32)


def nn_dot(a, b):
    return jnp.dot(a, b, preferred_element_type=jnp.float32)


def kernel(
    chips_z,
    plen_hbm, scount_hbm, slen_hbm, owner_hbm, dq_hbm, skv_hbm,
    prefix_hbm, pages_hbm, pq_hbm, pkv_hbm, w_hbm,
    dec, po,
    plen_ref, scount_ref, slen_ref, owner_ref, dq_ref, skv_ref,
    prefix, pages, pq, pkv, w, kt, v1,
    table, table_sib, tab_s, tab_sib_s,
    q_all, acc_send, st_send, acc_recv, st_recv, part, rs_recv,
    in_sem, tab_sem, swap_send, swap_recv,
    q_send, q_recv, a_send, a_recv, t_send, t_recv, r_send, r_recv,
):
    span = pq.shape[0]
    pages_dev = pages_hbm.shape[0]
    samples = dq_ref.shape[0]
    rows = samples * HEADS
    chips = q_all.shape[0]
    chips_y = chips // chips_z
    n_t = rs_recv.shape[0]
    dp = lax.axis_index("dp")
    me_t = lax.axis_index("tensor")
    chip, core = dp // 2, dp % 2
    sibling = chip * 2 + (1 - core)
    my_y, my_z = chip // chips_z, chip % chips_z

    early_waves, late_waves = list(range(chips_z // 2)), list(range(chips_z // 2, chips_z))
    is_first = my_z == 0
    is_early = my_z < chips_z // 2
    is_late = my_z >= chips_z // 2

    def chip_at(k, z):
        return ((my_y + k) % chips_y) * chips_z + z

    def remote(k, z, action):
        if k:
            action(chip_at(k, z))
        else:
            pl.when(my_z != z)(lambda: action(chip_at(k, z)))

    far_first = sorted(range(chips_y), key=lambda k: -min(k, chips_y - k))
    everywhere = [(k, z) for z in late_waves + early_waves for k in far_first]

    barrier = pltpu.get_barrier_semaphore()
    for k, z in everywhere:
        remote(k, z, lambda to: pl.semaphore_signal(
            barrier, inc=1, device_id=(to * 2 + core, me_t), device_id_type=MESH))
    for u in range(1, n_t):
        pl.semaphore_signal(barrier, inc=1, device_id=(dp, (me_t + u) % n_t), device_id_type=MESH)
    pl.semaphore_signal(barrier, inc=1, device_id=(sibling, me_t), device_id_type=MESH)

    load_kv = pltpu.make_async_copy(pkv_hbm, pkv, in_sem.at[0])
    load_q = pltpu.make_async_copy(pq_hbm, pq, in_sem.at[1])
    load_prefix = pltpu.make_async_copy(prefix_hbm.at[0], prefix, in_sem.at[2])
    load_pages = pltpu.make_async_copy(pages_hbm, pages.at[pl.ds(0, pages_dev)], in_sem.at[3])
    load_w = pltpu.make_async_copy(w_hbm, w, in_sem.at[4])
    small = [
        pltpu.make_async_copy(src, dst, in_sem.at[5 + i])
        for i, (src, dst) in enumerate((
            (owner_hbm, owner_ref), (slen_hbm, slen_ref), (dq_hbm, dq_ref), (skv_hbm, skv_ref),
            (plen_hbm, plen_ref), (scount_hbm, scount_ref)))
    ]
    load_owner, load_slen, load_dq, load_skv, load_plen, load_scount = small
    for copy in (load_owner, load_slen, load_kv, load_dq, load_q, load_pages, load_skv, load_plen, load_prefix,
                 load_scount, load_w):
        copy.start()

    load_owner.wait()
    prompts = table.shape[0]
    place = lax.broadcasted_iota(jnp.int32, (prompts, pages_dev), 1).astype(jnp.float32)
    prompt_at = lax.broadcasted_iota(jnp.int32, (prompts, pages_dev), 0)
    hit = jnp.broadcast_to(owner_ref[...], (prompts, pages_dev)) == prompt_at
    first = jnp.min(jnp.where(hit, place, float(pages_dev)), axis=1, keepdims=True)
    last = jnp.max(jnp.where(hit, place, -1.0), axis=1, keepdims=True)
    column = lax.broadcasted_iota(jnp.int32, (prompts, 128), 1)
    table[...] = jnp.where(column == 0, first, last).astype(jnp.int32)
    own_tab = pltpu.make_async_copy(table, tab_s, tab_sem.at[0])
    own_tab.start()

    block = min(BLOCK, span)
    n_blocks = span // block
    tri = lax.broadcasted_iota(jnp.int32, (block, block), 1) <= lax.broadcasted_iota(jnp.int32, (block, block), 0)

    def prepare():
        load_kv.wait()
        load_q.wait()
        load_slen.wait()
        ktt = pkv[:, :HD].T
        kt[:HD, :] = ktt
        kt[HD:, :] = ktt
        v1[:, :HD] = pkv[:, HD:]
        v1[:, HD:] = jnp.ones((span, HD), jnp.bfloat16)

    def scores(i, h):
        lo, nk = i * block, (i + 1) * block
        q = pq[lo:nk, h * HD:(h + 1) * HD].astype(jnp.float32) * SCALE
        q_hi = q.astype(jnp.bfloat16)
        q_lo = (q - q_hi.astype(jnp.float32)).astype(jnp.bfloat16)
        return nn_dot(jnp.concatenate([q_hi, q_lo], axis=1), kt[:, :nk])

    def finish(i, h, s):
        lo, nk = i * block, (i + 1) * block
        diag = jnp.where(tri, s[:, lo:], NEG)
        s = jnp.concatenate([s[:, :lo], diag], axis=1) if i else diag
        top = jnp.max(s, axis=1, keepdims=True)
        p = jnp.exp2(s - top).astype(jnp.bfloat16)
        o = nn_dot(p, v1[:nk, :])
        live = lo + lax.broadcasted_iota(jnp.int32, (block, HD), 0) < jnp.broadcast_to(slen_ref[...], (block, HD))
        out = jnp.where(live, o[:, :HD] / o[:, HD:], 0.0)
        po[lo:nk, h * HD:(h + 1) * HD] = out.astype(jnp.bfloat16)

    def prefill(*blocks):
        units = [(i, h) for i in blocks for h in range(HEADS)]
        s = scores(*units[0])
        for unit, later in zip(units, units[1:] + [None]):
            ahead = scores(*later) if later else None
            finish(*unit, s)
            s = ahead

    prepare()
    prefill(0, 1)

    pl.semaphore_wait(barrier, chips - 1 + n_t - 1 + 1)
    load_dq.wait()
    swap = [
        pltpu.make_async_remote_copy(
            table, table_sib, swap_send.at[0], swap_recv.at[0], device_id=(sibling, me_t), device_id_type=MESH),
        pltpu.make_async_remote_copy(
            pages_hbm, pages.at[pl.ds(pages_dev, pages_dev)], swap_send.at[1], swap_recv.at[1],
            device_id=(sibling, me_t), device_id_type=MESH),
    ]

    def q_copy(to, slot):
        return pltpu.make_async_remote_copy(
            dq_ref, q_all.at[slot], q_send.at[to], q_recv.at[slot],
            device_id=(to * 2 + core, me_t), device_id_type=MESH)

    def send_queries():
        for k, z in everywhere:
            remote(k, z, lambda to: q_copy(to, chip).start())

    swap[0].start()
    send_queries()
    swap[1].start()
    q_all[chip] = dq_ref[...]

    def stacked(x):
        return jnp.concatenate([x[:, h * HD:(h + 1) * HD] for h in range(HEADS)], axis=0)

    dq = stacked(dq_ref[...])
    load_prefix.wait()
    load_skv.wait()
    load_plen.wait()
    n_prefix = prefix.shape[0]
    s = nt_dot(dq, prefix[:, :HD]) * SCALE
    at = lax.broadcasted_iota(jnp.int32, (rows, n_prefix), 1)
    s = jnp.where(at < jnp.broadcast_to(plen_ref[...], (rows, n_prefix)), s, NEG)
    own_k = jnp.concatenate([skv_ref[:, :HD].astype(jnp.float32)] * HEADS, axis=0)
    own_v = jnp.concatenate([skv_ref[:, HD:].astype(jnp.float32)] * HEADS, axis=0)
    own_s = jnp.sum(dq.astype(jnp.float32) * own_k, axis=1, keepdims=True) * SCALE
    m_pre = jnp.maximum(jnp.max(s, axis=1, keepdims=True), own_s)
    p = jnp.exp2(s - m_pre)
    own_w = jnp.exp2(own_s - m_pre)
    l_pre = jnp.sum(p, axis=1, keepdims=True) + own_w
    acc_pre = nn_dot(p.astype(jnp.bfloat16), prefix[:, HD:])
    acc_pre = acc_pre + own_w.astype(jnp.bfloat16).astype(jnp.float32) * own_v

    prefill(2, 3, 4)

    load_pages.wait()
    own_tab.wait()
    swap[0].wait()
    sib_tab = pltpu.make_async_copy(table_sib, tab_sib_s, tab_sem.at[1])
    sib_tab.start()
    sib_tab.wait()
    swap[1].wait()
    ones = jnp.ones((pages.shape[1], HD), jnp.bfloat16)
    lane_r = lax.broadcasted_iota(jnp.int32, (rows, 128), 1)
    row_r = lax.broadcasted_iota(jnp.int32, (rows, 128), 0)

    def a_copy(to, slot):
        return pltpu.make_async_remote_copy(
            acc_send.at[to], acc_recv.at[slot], a_send.at[to], a_recv.at[slot],
            device_id=(to * 2 + core, me_t), device_id_type=MESH)

    def t_copy(to, slot):
        return pltpu.make_async_remote_copy(
            st_send.at[to], st_recv.at[slot], t_send.at[to], t_recv.at[slot],
            device_id=(to * 2 + core, me_t), device_id_type=MESH)

    def serve(r):
        q = stacked(q_all[r])
        prompt = r * 2 + core
        held = []
        for tab, base in ((tab_s, 0), (tab_sib_s, pages_dev)):
            a, b = tab[prompt, 0], tab[prompt, 1]
            held.append((base + jnp.clip(a, 0, pages_dev - 1), b >= a))
            held.append((base + jnp.clip(b, 0, pages_dev - 1), b > a))
        kvs = [pages[index] for index, _ in held]
        s = jnp.concatenate(
            [nt_dot(q, kv[:, :HD]) * SCALE + jnp.where(valid, 0.0, NEG)
             for kv, (_, valid) in zip(kvs, held)], axis=1)
        m = jnp.max(s, axis=1, keepdims=True)
        p = jnp.exp2(s - m).astype(jnp.bfloat16)
        v = jnp.concatenate([jnp.concatenate([kv[:, HD:], ones], axis=1) for kv in kvs], axis=0)
        o = nn_dot(p, v)
        stat = jnp.where(lane_r == row_r, m, jnp.where(lane_r == row_r + rows, o[:, HD:], 0.0))
        stat = jnp.sum(stat, axis=0, keepdims=True)
        acc_send[r] = o[:, :HD].astype(jnp.bfloat16)
        st_send[r] = stat

    for z in early_waves + late_waves:
        for k in far_first:
            remote(k, z, lambda of: q_copy(of, of).wait_recv())
        for k in far_first:
            serve(chip_at(k, z))
        for k in far_first:
            remote(k, z, lambda to: t_copy(to, chip).start())
            remote(k, z, lambda to: a_copy(to, chip).start())
    acc_recv[chip] = acc_send[chip]
    st_recv[chip] = st_send[chip]
    prefill(5, 7)

    for k, z in everywhere:
        remote(k, z, lambda of: t_copy(of, of).wait_recv())
        remote(k, z, lambda of: a_copy(of, of).wait_recv())
    stats = jnp.concatenate([st_recv[r] for r in range(chips)], axis=0).T
    m_all, l_all = stats[:rows, :], stats[rows:2 * rows, :]
    m_top = jnp.maximum(jnp.max(m_all, axis=1, keepdims=True), m_pre)
    w_all = jnp.exp2(m_all - m_top)
    w_pre = jnp.exp2(m_pre - m_top)
    total = jnp.sum(l_all * w_all, axis=1, keepdims=True) + l_pre * w_pre
    acc = acc_pre * w_pre
    for r in range(chips):
        acc = acc + acc_recv[r].astype(jnp.float32) * w_all[:, r:r + 1]
    att = (acc / total).astype(jnp.bfloat16)
    att = jnp.concatenate([att[h * samples:(h + 1) * samples, :] for h in range(HEADS)], axis=1)

    load_w.wait()
    wide = dec.shape[1]

    def product(u):
        to = (me_t + u) % n_t
        return nn_dot(att, w[:, pl.ds(pl.multiple_of(to * wide, wide), wide)])

    def r_copy(u):
        return pltpu.make_async_remote_copy(
            part.at[u], rs_recv.at[u], r_send.at[u], r_recv.at[u],
            device_id=(dp, (me_t + u) % n_t), device_id_type=MESH)

    for u in range(1, n_t):
        part[u] = product(u).astype(jnp.bfloat16)
        r_copy(u).start()
    part[0] = product(0).astype(jnp.bfloat16)

    prefill(6)

    sums = part[0].astype(jnp.float32)
    for u in range(1, n_t):
        r_copy(u).wait_recv()
        sums = sums + rs_recv[u].astype(jnp.float32)
    load_scount.wait()
    alive = lax.broadcasted_iota(jnp.int32, sums.shape, 0) < jnp.broadcast_to(scount_ref[...], sums.shape)
    dec[...] = jnp.where(alive, sums, 0.0).astype(jnp.bfloat16)

    for k, z in everywhere:
        remote(k, z, lambda to: q_copy(to, chip).wait_send())
        remote(k, z, lambda to: t_copy(to, chip).wait_send())
        remote(k, z, lambda to: a_copy(to, chip).wait_send())
    for u in range(1, n_t):
        r_copy(u).wait_send()


def store(dec, pre, dec_out, pre_out, sem):
    copies = [pltpu.make_async_copy(pre, pre_out, sem.at[0]), pltpu.make_async_copy(dec, dec_out, sem.at[1])]
    for copy in copies:
        copy.start()
    for copy in copies:
        copy.wait()


def solution(mesh, chips_z=GRID_Z):
    chips = mesh.shape["dp"] // 2
    n_t = mesh.shape["tensor"]

    def body(prefix_cache, prefix_len, decode_q, sample_kv, sample_count, sectioned_pages, page_owner,
             prefill_q, prefill_kv, span_len, out_weight):
        n_prefix, wide_kv = prefix_cache.shape[1:]
        pages_dev, page, _ = sectioned_pages.shape
        span, wide_q = prefill_q.shape
        samples = decode_q.shape[0]
        rows = samples * HEADS
        features = out_weight.shape[1]
        bf, f32 = jnp.bfloat16, jnp.float32
        hbm = pl.BlockSpec(memory_space=pltpu.HBM)
        prompts = mesh.shape["dp"]
        dma, vm = pltpu.SemaphoreType.DMA, pltpu.VMEM
        outs = pl.pallas_call(
            functools.partial(kernel, chips_z),
            out_shape=(
                vm((samples, features // n_t), bf),
                vm((span, wide_q), bf),
            ),
            in_specs=[hbm] * 11,
            out_specs=(pl.BlockSpec(memory_space=vm),) * 2,
            scratch_shapes=[
                vm((1, 1), jnp.int32), vm((1, 1), jnp.int32), vm((1, 1), jnp.int32),
                vm((1, pages_dev), jnp.int32), vm((samples, wide_q), bf), vm((samples, wide_kv), bf),
                vm((n_prefix, wide_kv), bf), vm((2 * pages_dev, page, wide_kv), bf),
                vm((span, wide_q), bf), vm((span, wide_kv), bf), vm(out_weight.shape, bf),
                vm((2 * HD, span), bf), vm((span, 2 * HD), bf),
                vm((prompts, 128), jnp.int32), vm((prompts, 128), jnp.int32),
                pltpu.SMEM((prompts, 128), jnp.int32), pltpu.SMEM((prompts, 128), jnp.int32),
                vm((chips, samples, wide_q), bf), vm((chips, rows, HD), bf), vm((chips, 1, 128), f32),
                vm((chips, rows, HD), bf), vm((chips, 1, 128), f32),
                vm((n_t, samples, features // n_t), bf), vm((n_t, samples, features // n_t), bf),
                dma((11,)), dma((2,)), dma((2,)), dma((2,)),
                dma((chips,)), dma((chips,)), dma((chips,)), dma((chips,)), dma((chips,)), dma((chips,)),
                dma((n_t,)), dma((n_t,)),
            ],
            compiler_params=pltpu.CompilerParams(
                collective_id=0, has_side_effects=True, vmem_limit_bytes=56 * 2**20),
            cost_estimate=pl.CostEstimate(flops=6 * 10**9, bytes_accessed=12 * 2**20, transcendentals=10**7),
        )(prefix_len[None], sample_count[None], span_len[None], page_owner.T, decode_q, sample_kv,
          prefix_cache, sectioned_pages, prefill_q, prefill_kv, out_weight)
        return pl.pallas_call(
            store,
            out_shape=tuple(jax.ShapeDtypeStruct(out.shape, out.dtype) for out in outs),
            in_specs=[pl.BlockSpec(memory_space=vm)] * 2,
            out_specs=(hbm, hbm),
            scratch_shapes=[dma((2,))],
        )(*(pltpu.with_memory_space_constraint(out, vm) for out in outs))

    in_specs = (
        P("dp", None, "tensor"), P("dp"), P("dp", "tensor"), P("dp", "tensor"), P("dp"),
        P("dp", None, "tensor"), P("dp", None), P("dp", "tensor"), P("dp", "tensor"), P("dp"), P("tensor", None),
    )
    out_specs = (P("dp", "tensor"), P("dp", "tensor"))
    return jax.shard_map(body, mesh=mesh, in_specs=in_specs, out_specs=out_specs, check_vma=False)
```
